32 devices in a mesh: ctx: 8 (over z, y), head: 4 (over x, core).
Axes of the slice: x: 2, y: 2, z: 4, core: 2. Of those that a mesh axis runs over, the one named last changes fastest.
Arguments:
- tokens: bfloat16 [4096, 2048], P('ctx'), may hold values from -6 to 6
- w_proj: bfloat16 [2048, 10240], P('ctx', 'head'), may hold values from -0.125 to 0.125
- w_small: bfloat16 [2048, 48], P('ctx', 'head'), may hold values from -0.125 to 0.125
- beta_bias: float32 [16, 2], P('head'), may hold values from 5 to 9
- decay_rate: float32 [16], P('head'), may hold values from 5e-07 to 0.05
- w_out: bfloat16 [2048, 2048], P('head', 'ctx'), may hold values from -0.125 to 0.125
Outputs:
- mixed: bfloat16 [4096, 2048], P(('ctx', 'head'))
The draws below stay inside these ranges and needn't reach their ends.
All inputs are finite; a program needn't handle non-finite values.
Results may differ from the reference program's by a relative error of at most 0.006.
Values may be sent and summed in bfloat16 or wider, within the bound.
A program may use at most 128 MiB of HBM per device.

```python
import math
import jax
import jax.numpy as jnp
from jax import lax

D = 2048
HEADS = 16
DK = 128
REFLECTIONS = 2
TOKENS = 4096


def draw_decay_rate(key, part):
    uniform_part = jax.random.uniform(key, (HEADS,), jnp.float32)
    lowest = math.log(5e-07)
    upper_end = math.log(0.05)
    return jnp.exp(lowest + uniform_part * (upper_end - lowest))


def steps_of(own_key, dims, pieces, low, top_value):
    loudness = 1.0
    for axis_at, shards_of in pieces:
        heights = jax.random.uniform(jax.random.fold_in(jax.random.fold_in(own_key, 6), axis_at), (shards_of,), jnp.float32, low / len(pieces), top_value / len(pieces))
        loudness = loudness * jnp.repeat(jnp.exp(heights), dims[axis_at] // shards_of).reshape((-1,) + (1,) * (len(dims) - 1 - axis_at))
    return loudness


def noise(key, dims, spread, most, cuts=(), dtype=jnp.bfloat16):
    result = spread * jax.random.normal(key, dims, jnp.float32)
    if cuts:
        result = result * steps_of(key, dims, cuts, -0.22, 0.18)
    return jnp.clip(result, -most, most).astype(dtype)


def setup_inputs(seed: int = 0) -> dict:
    splits = jax.random.split(jax.random.key(seed), 7)
    return {
        "tokens": noise(splits[0], (TOKENS, D), 1.0, 6.0, ((0, 8),)),
        "w_proj": noise(splits[1], (D, HEADS * (1 + 2 * REFLECTIONS) * DK), D ** -0.5, 0.125, ((0, 8), (1, 4))),
        "w_small": noise(splits[2], (D, HEADS * (REFLECTIONS + 1)), D ** -0.5, 0.125, ((0, 8), (1, 4))),
        "beta_bias": jnp.clip(5.0 + 4.0 * jax.random.uniform(splits[3], (HEADS, REFLECTIONS), jnp.float32) ** steps_of(splits[3], (HEADS, REFLECTIONS), ((0, 4),), -0.2, 0.2), 5.0, 9.0),
        "decay_rate": draw_decay_rate(jax.random.fold_in(splits[6], 71), 0),
        "w_out": noise(splits[5], (HEADS * DK, D), (HEADS * DK) ** -0.5, 0.125, ((0, 4), (1, 8))),
    }


HIGHEST_PRECISION = lax.Precision.HIGHEST

def unit_rows(vectors):
    return vectors / jnp.sqrt(lax.optimization_barrier(jnp.sum(vectors * vectors, axis=-1, keepdims=True)) + 1e-06)

def reference(tokens, w_proj, w_small, beta_bias, decay_rate, w_out):
    block_rows = math.gcd(TOKENS, 256)
    blocks = TOKENS // block_rows
    mirrors = REFLECTIONS

    def token_step(state, inputs):
        query, keys, values, betas, decay = inputs
        state = decay[:, None, None] * state
        for index in range(mirrors):
            key_now = keys[:, index]
            recalled = jnp.einsum('hab,hb->ha', state, key_now, precision=HIGHEST_PRECISION)
            change = (values[:, index] - recalled) * betas[:, index, None]
            state = state + change[:, :, None] * key_now[:, None, :]
        return (state, jnp.einsum('hab,hb->ha', state, query, precision=HIGHEST_PRECISION))

    def block_step(state, rows):
        projected = jnp.dot(rows, w_proj, preferred_element_type=jnp.float32)
        gate_inputs = jnp.dot(rows, w_small, preferred_element_type=jnp.float32)
        parts = projected.reshape(block_rows, HEADS, 1 + 2 * mirrors, DK)
        queries = unit_rows(parts[:, :, 0])
        keys_all = unit_rows(parts[:, :, 1:1 + mirrors])
        values_all = parts[:, :, 1 + mirrors:]
        gate_cols = gate_inputs.reshape(block_rows, HEADS, mirrors + 1)
        betas = 2.0 * jax.nn.sigmoid(gate_cols[:, :, :mirrors] + beta_bias[None])
        decay = jnp.exp(-decay_rate[None, :] * jax.nn.softplus(gate_cols[:, :, mirrors]))
        state, head_out = lax.scan(token_step, state, (queries, keys_all, values_all, betas, decay))
        normed = head_out / jnp.sqrt(lax.optimization_barrier(jnp.mean(head_out * head_out, axis=-1, keepdims=True)) + 1e-06)
        normed = normed.astype(jnp.bfloat16).reshape(block_rows, HEADS * DK)
        return (state, jnp.dot(normed, w_out, preferred_element_type=jnp.float32).astype(jnp.bfloat16))
    start = jnp.zeros((HEADS, DK, DK), jnp.float32)
    final_state, mixed = lax.scan(block_step, start, tokens.reshape(blocks, block_rows, D))
    return mixed.reshape(TOKENS, D)
```

```python
import functools
import math

import jax
import jax.numpy as jnp
from jax import lax
from jax.experimental import pallas as pl
from jax.experimental.pallas import tpu as pltpu
from jax.sharding import PartitionSpec as P

F32 = jnp.float32
BF16 = jnp.bfloat16
NN = (((1,), (0,)), ((), ()))
NT = (((1,), (1,)), ((), ()))
TN = (((0,), (0,)), ((), ()))
BLOCK = 64
BASE = 8


def dot1(left, right, dims=NN):
    return lax.dot_general(left, right, dims, preferred_element_type=F32)


def halves(array):
    high = array.astype(BF16)
    return high, (array - high.astype(F32)).astype(BF16)


def dot3(left, right, dims=NN):
    left_high, left_low = halves(left)
    right_high, right_low = halves(right)
    return (
        dot1(left_high, right_high, dims)
        + dot1(left_high, right_low, dims)
        + dot1(left_low, right_high, dims)
    )


def unit(vectors):
    return vectors * lax.rsqrt(jnp.sum(vectors * vectors, axis=-1, keepdims=True) + 1e-06)


def chunk_kernel(heads, mirrors, width, proj_ref, gate_ref, bias_ref, rate_ref, pre_ref, reach_ref, total_ref):
    toks = proj_ref.shape[0]
    span = toks * mirrors
    parts = 1 + 2 * mirrors
    gates = mirrors + 1

    @pl.when(pl.program_id(0) == 0)
    def _():
        rows = lax.broadcasted_iota(jnp.int32, (2 * width, width), 0)
        cols = lax.broadcasted_iota(jnp.int32, (2 * width, width), 1)
        start = jnp.where(rows == cols, 1.0, 0.0).astype(F32)
        for head in range(heads):
            total_ref[head] = start

    gate = gate_ref[...]
    strength = 2.0 / (1.0 + jnp.exp(-(gate + bias_ref[...])))
    log_decay = -rate_ref[...] * (jnp.maximum(gate, 0.0) + jnp.log(1.0 + jnp.exp(-jnp.abs(gate))))
    tok_r = lax.broadcasted_iota(jnp.int32, (toks, toks), 0)
    tok_c = lax.broadcasted_iota(jnp.int32, (toks, toks), 1)
    upto = jnp.where(tok_r >= tok_c, 1.0, 0.0).astype(F32)
    summed = lax.dot_general(
        upto, log_decay, NN, precision=lax.Precision.HIGHEST, preferred_element_type=F32
    )
    step_r = lax.broadcasted_iota(jnp.int32, (span, span), 0)
    step_c = lax.broadcasted_iota(jnp.int32, (span, span), 1)
    place_r = (step_r % toks) * mirrors + step_r // toks
    place_c = (step_c % toks) * mirrors + step_c // toks
    strict = place_r > place_c
    diagonal = step_r == step_c
    eye = jnp.where(diagonal, 1.0, 0.0).astype(F32)
    see_r = lax.broadcasted_iota(jnp.int32, (toks, span), 0)
    see_c = lax.broadcasted_iota(jnp.int32, (toks, span), 1)
    visible = see_c % toks <= see_r

    each = range(heads)

    def part(head, index):
        at = (head * parts + index) * width
        return proj_ref[:, at : at + width]

    query = [unit(part(h, 0)) for h in each]
    keys = [jnp.concatenate([unit(part(h, 1 + r)) for r in range(mirrors)], axis=0) for h in each]
    values = [jnp.concatenate([part(h, 1 + mirrors + r) for r in range(mirrors)], axis=0) for h in each]
    beta = [
        jnp.concatenate([strength[:, h * gates + r : h * gates + r + 1] for r in range(mirrors)], axis=0)
        for h in each
    ]
    run_q = [summed[:, h * gates + mirrors : h * gates + mirrors + 1] for h in each]
    run = [jnp.concatenate([run_q[h]] * mirrors, axis=0) for h in each]
    run_row = [jnp.sum(jnp.where(diagonal, run[h], 0.0), axis=0, keepdims=True) for h in each]
    last = [run_q[h][toks - 1 :, :] for h in each]
    inner = [dot3(jnp.concatenate([keys[h], query[h]], axis=0), keys[h], NT) for h in each]
    lower = [
        jnp.where(strict, beta[h] * jnp.exp(jnp.where(strict, run[h] - run_row[h], 0.0)) * inner[h][:span], 0.0)
        for h in each
    ]
    attend = [
        jnp.where(visible, jnp.exp(jnp.where(visible, run_q[h] - run_row[h], 0.0)) * inner[h][span:], 0.0)
        for h in each
    ]
    low_high = [halves(lower[h]) for h in each]
    near = place_r // BASE == place_c // BASE
    zero = jnp.zeros((), BF16)
    power = [jnp.where(near, low_high[h][0], zero) for h in each]
    inv = [eye - jnp.where(near, lower[h], 0.0) for h in each]
    reached = 2
    while reached < BASE:
        power = [dot1(power[h], power[h]).astype(BF16) for h in each]
        inv = [inv[h] + dot1(inv[h].astype(BF16), power[h]) for h in each]
        reached *= 2
    size = BASE
    while size < span:
        joined = (place_r // (2 * size) == place_c // (2 * size)) & (place_r // size != place_c // size)
        inv_now = [inv[h].astype(BF16) for h in each]
        cross = [dot1(jnp.where(joined, low_high[h][0], zero), inv_now[h]).astype(BF16) for h in each]
        inv = [inv[h] - dot1(inv_now[h], cross[h]) for h in each]
        size *= 2
    rough = [inv[h].astype(BF16) for h in each]
    left = [
        (eye - rough[h].astype(F32)) - dot1(low_high[h][0], rough[h]) - dot1(low_high[h][1], rough[h])
        for h in each
    ]
    inv = [rough[h].astype(F32) + dot1(rough[h], left[h].astype(BF16)) for h in each]

    given = [
        jnp.concatenate([beta[h] * values[h], (beta[h] * jnp.exp(run[h])) * keys[h]], axis=1) for h in each
    ]
    weighted = [dot3(inv[h], given[h]) for h in each]
    tails = [jnp.exp(last[h] - run[h]) * keys[h] for h in each]
    moved = [dot3(weighted[h], tails[h], TN) for h in each]
    seen = [dot3(attend[h], weighted[h]) for h in each]
    asked = [jnp.exp(run_q[h]) * query[h] - seen[h][:, width:] for h in each]
    before = [total_ref[h] for h in each]
    answers = [dot3(asked[h], before[h], NT) for h in each]
    after = [dot3(before[h], moved[h][width:]) for h in each]
    for h in each:
        reach_ref[:, h * width : (h + 1) * width] = answers[h][:, :width]
        pre_ref[:, h * width : (h + 1) * width] = answers[h][:, width:] + seen[h][:, :width]
        carried = jnp.exp(last[h]) * before[h] - after[h]
        total_ref[h, :width] = carried[:width]
        total_ref[h, width:] = carried[width:] + moved[h][:width]


def chunk_call(projected, gate_inputs, bias_row, rate_row, heads, mirrors, width, interpret=False):
    toks = projected.shape[0]
    block = math.gcd(toks, BLOCK)
    gates = gate_inputs.shape[1]
    span = block * mirrors
    units = toks // block * heads
    return pl.pallas_call(
        functools.partial(chunk_kernel, heads, mirrors, width),
        grid=(toks // block,),
        in_specs=[
            pl.BlockSpec((block, projected.shape[1]), lambda i: (i, 0)),
            pl.BlockSpec((block, gates), lambda i: (i, 0)),
            pl.BlockSpec((1, gates), lambda i: (0, 0)),
            pl.BlockSpec((1, gates), lambda i: (0, 0)),
        ],
        out_specs=[
            pl.BlockSpec((block, heads * width), lambda i: (i, 0)),
            pl.BlockSpec((block, heads * width), lambda i: (i, 0)),
            pl.BlockSpec((heads, 2 * width, width), lambda i: (0, 0, 0)),
        ],
        out_shape=[
            jax.ShapeDtypeStruct((toks, heads * width), F32),
            jax.ShapeDtypeStruct((toks, heads * width), F32),
            jax.ShapeDtypeStruct((heads, 2 * width, width), F32),
        ],
        compiler_params=pltpu.CompilerParams(vmem_limit_bytes=48 * 2**20),
        cost_estimate=pl.CostEstimate(
            flops=2 * units * 60 * span * span * width, bytes_accessed=4 * projected.size, transcendentals=0
        ),
        interpret=interpret,
    )(projected, gate_inputs, bias_row, rate_row)


def finish_kernel(heads, width, pre_ref, reach_ref, state_ref, out_ref):
    for head in range(heads):
        cols = slice(head * width, (head + 1) * width)
        out = pre_ref[:, cols] + dot3(reach_ref[:, cols], state_ref[head], NT)
        scale = lax.rsqrt(jnp.mean(out * out, axis=-1, keepdims=True) + 1e-06)
        out_ref[:, cols] = (out * scale).astype(BF16)


def finish_call(pre, reach, state, heads, width, interpret=False):
    return pl.pallas_call(
        functools.partial(finish_kernel, heads, width),
        out_shape=jax.ShapeDtypeStruct(pre.shape, BF16),
        compiler_params=pltpu.CompilerParams(vmem_limit_bytes=32 * 2**20),
        cost_estimate=pl.CostEstimate(
            flops=6 * pre.size * width, bytes_accessed=10 * pre.size, transcendentals=0
        ),
        interpret=interpret,
    )(pre, reach, state)


def from_behind(array, axis, by):
    count = lax.axis_size(axis)
    pairs = [(i, i + by) for i in range(count) if 0 <= i + by < count]
    return lax.ppermute(array, axis, pairs)


def matrix_product(left, right):
    return jnp.matmul(left, right, precision=lax.Precision.HIGHEST)


def gate_rows(beta_bias, decay_rate):
    heads, mirrors = beta_bias.shape
    bias = jnp.concatenate([beta_bias, jnp.zeros((heads, 1), F32)], axis=1).reshape(1, -1)
    rate = jnp.concatenate([jnp.zeros((heads, mirrors), F32), decay_rate[:, None]], axis=1).reshape(1, -1)
    return bias, rate


def shards(tokens, w_proj, w_small, beta_bias, decay_rate, w_out):
    tok_rows = tokens.shape[0]
    heads_here, mirrors = beta_bias.shape
    head_width = w_proj.shape[1] // (heads_here * (1 + 2 * mirrors))
    wide = w_proj.shape[1]
    fill = -w_small.shape[1] % 128
    both = jnp.concatenate([w_proj, jnp.pad(w_small, ((0, 0), (0, fill)))], axis=1)
    both = lax.all_gather(both, "ctx", axis=0, tiled=True)
    projected = jnp.dot(tokens, both, preferred_element_type=F32)
    later_out, projected = lax.optimization_barrier((w_out, projected))
    gate_inputs = projected[:, wide : wide + w_small.shape[1]]
    projected = projected[:, :wide]
    bias_row, rate_row = gate_rows(beta_bias, decay_rate)
    pre, reach, total = chunk_call(
        projected, gate_inputs, bias_row, rate_row, heads_here, mirrors, head_width
    )
    device_trans = total[:, :head_width]
    device_write = total[:, head_width:]

    def relay(turn, incoming):
        outgoing = matrix_product(incoming, device_trans) + device_write
        return from_behind(outgoing, "ctx", 1)

    state_in = lax.fori_loop(
        0, lax.axis_size("ctx") - 1, relay, jnp.zeros(device_write.shape, F32)
    )
    mixed_heads = finish_call(pre, reach, state_in, heads_here, head_width)
    grouped = lax.all_gather(later_out, "head", axis=0, tiled=True)
    full_out = lax.all_gather(grouped, "ctx", axis=1, tiled=True)
    group_count = lax.axis_size("head")
    rows_each = tok_rows // group_count
    stacked = mixed_heads.reshape(group_count, rows_each, heads_here * head_width)
    mixed = jnp.einsum(
        "irk,kd->ird",
        lax.all_to_all(stacked, "head", split_axis=0, concat_axis=2, tiled=True),
        full_out,
        preferred_element_type=F32,
    ).astype(BF16)
    return mixed.reshape(rows_each, full_out.shape[1])


def solution(mesh):
    placed = (
        P("ctx", None),
        P("ctx", "head"),
        P("ctx", "head"),
        P("head", None),
        P("head"),
        P("head", "ctx"),
    )
    return jax.shard_map(
        shards, mesh=mesh, in_specs=placed, out_specs=P(("ctx", "head"), None), check_vma=False
    )
```

```python
import functools
import math

import jax
import jax.numpy as jnp
from jax import lax
from jax.experimental import pallas as pl
from jax.experimental.pallas import tpu as pltpu
from jax.sharding import PartitionSpec as P

F32 = jnp.float32
BF16 = jnp.bfloat16
NN = (((1,), (0,)), ((), ()))
NT = (((1,), (1,)), ((), ()))
TN = (((0,), (0,)), ((), ()))
BLOCK = 64
BASE = 8


def dot1(left, right, dims=NN):
    return lax.dot_general(left, right, dims, preferred_element_type=F32)


def halves(array):
    high = array.astype(BF16)
    return high, (array - high.astype(F32)).astype(BF16)


def dot3(left, right, dims=NN):
    left_high, left_low = halves(left)
    right_high, right_low = halves(right)
    return (
        dot1(left_high, right_high, dims)
        + dot1(left_high, right_low, dims)
        + dot1(left_low, right_high, dims)
    )


def unit(vectors):
    return vectors * lax.rsqrt(jnp.sum(vectors * vectors, axis=-1, keepdims=True) + 1e-06)


def chunk_kernel(heads, mirrors, width, proj_ref, gate_ref, bias_ref, rate_ref, pre_ref, reach_ref, total_ref):
    toks = proj_ref.shape[0]
    span = toks * mirrors
    parts = 1 + 2 * mirrors
    gates = mirrors + 1

    @pl.when(pl.program_id(0) == 0)
    def _():
        rows = lax.broadcasted_iota(jnp.int32, (2 * width, width), 0)
        cols = lax.broadcasted_iota(jnp.int32, (2 * width, width), 1)
        start = jnp.where(rows == cols, 1.0, 0.0).astype(F32)
        for head in range(heads):
            total_ref[head] = start

    gate = gate_ref[...]
    strength = 2.0 / (1.0 + jnp.exp(-(gate + bias_ref[...])))
    log_decay = -rate_ref[...] * (jnp.maximum(gate, 0.0) + jnp.log(1.0 + jnp.exp(-jnp.abs(gate))))
    tok_r = lax.broadcasted_iota(jnp.int32, (toks, toks), 0)
    tok_c = lax.broadcasted_iota(jnp.int32, (toks, toks), 1)
    upto = jnp.where(tok_r >= tok_c, 1.0, 0.0).astype(F32)
    summed = lax.dot_general(
        upto, log_decay, NN, precision=lax.Precision.HIGHEST, preferred_element_type=F32
    )
    step_r = lax.broadcasted_iota(jnp.int32, (span, span), 0)
    step_c = lax.broadcasted_iota(jnp.int32, (span, span), 1)
    place_r = (step_r % toks) * mirrors + step_r // toks
    place_c = (step_c % toks) * mirrors + step_c // toks
    strict = place_r > place_c
    diagonal = step_r == step_c
    eye = jnp.where(diagonal, 1.0, 0.0).astype(F32)
    see_r = lax.broadcasted_iota(jnp.int32, (toks, span), 0)
    see_c = lax.broadcasted_iota(jnp.int32, (toks, span), 1)
    visible = see_c % toks <= see_r

    each = range(heads)

    def part(head, index):
        at = (head * parts + index) * width
        return proj_ref[:, at : at + width]

    query = [unit(part(h, 0)) for h in each]
    keys = [jnp.concatenate([unit(part(h, 1 + r)) for r in range(mirrors)], axis=0) for h in each]
    values = [jnp.concatenate([part(h, 1 + mirrors + r) for r in range(mirrors)], axis=0) for h in each]
    beta = [
        jnp.concatenate([strength[:, h * gates + r : h * gates + r + 1] for r in range(mirrors)], axis=0)
        for h in each
    ]
    run_q = [summed[:, h * gates + mirrors : h * gates + mirrors + 1] for h in each]
    run = [jnp.concatenate([run_q[h]] * mirrors, axis=0) for h in each]
    run_row = [jnp.sum(jnp.where(diagonal, run[h], 0.0), axis=0, keepdims=True) for h in each]
    last = [run_q[h][toks - 1 :, :] for h in each]
    inner = [dot3(jnp.concatenate([keys[h], query[h]], axis=0), keys[h], NT) for h in each]
    lower = [
        jnp.where(strict, beta[h] * jnp.exp(jnp.where(strict, run[h] - run_row[h], 0.0)) * inner[h][:span], 0.0)
        for h in each
    ]
    attend = [
        jnp.where(visible, jnp.exp(jnp.where(visible, run_q[h] - run_row[h], 0.0)) * inner[h][span:], 0.0)
        for h in each
    ]
    low_high = [halves(lower[h]) for h in each]
    near = place_r // BASE == place_c // BASE
    zero = jnp.zeros((), BF16)
    power = [jnp.where(near, low_high[h][0], zero) for h in each]
    inv = [eye - jnp.where(near, lower[h], 0.0) for h in each]
    reached = 2
    while reached < BASE:
        power = [dot1(power[h], power[h]).astype(BF16) for h in each]
        inv = [inv[h] + dot1(inv[h].astype(BF16), power[h]) for h in each]
        reached *= 2
    size = BASE
    while size < span:
        joined = (place_r // (2 * size) == place_c // (2 * size)) & (place_r // size != place_c // size)
        inv_now = [inv[h].astype(BF16) for h in each]
        cross = [dot1(jnp.where(joined, low_high[h][0], zero), inv_now[h]).astype(BF16) for h in each]
        inv = [inv[h] - dot1(inv_now[h], cross[h]) for h in each]
        size *= 2
    rough = [inv[h].astype(BF16) for h in each]
    left = [
        (eye - rough[h].astype(F32)) - dot1(low_high[h][0], rough[h]) - dot1(low_high[h][1], rough[h])
        for h in each
    ]
    inv = [rough[h].astype(F32) + dot1(rough[h], left[h].astype(BF16)) for h in each]

    given = [
        jnp.concatenate([beta[h] * values[h], (beta[h] * jnp.exp(run[h])) * keys[h]], axis=1) for h in each
    ]
    weighted = [dot3(inv[h], given[h]) for h in each]
    tails = [jnp.exp(last[h] - run[h]) * keys[h] for h in each]
    moved = [dot3(weighted[h], tails[h], TN) for h in each]
    seen = [dot3(attend[h], weighted[h]) for h in each]
    asked = [jnp.exp(run_q[h]) * query[h] - seen[h][:, width:] for h in each]
    before = [total_ref[h] for h in each]
    answers = [dot3(asked[h], before[h], NT) for h in each]
    after = [dot3(before[h], moved[h][width:]) for h in each]
    for h in each:
        reach_ref[:, h * width : (h + 1) * width] = answers[h][:, :width]
        pre_ref[:, h * width : (h + 1) * width] = answers[h][:, width:] + seen[h][:, :width]
        carried = jnp.exp(last[h]) * before[h] - after[h]
        total_ref[h, :width] = carried[:width]
        total_ref[h, width:] = carried[width:] + moved[h][:width]


def chunk_call(projected, gate_inputs, bias_row, rate_row, heads, mirrors, width, interpret=False):
    toks = projected.shape[0]
    block = math.gcd(toks, BLOCK)
    gates = gate_inputs.shape[1]
    span = block * mirrors
    units = toks // block * heads
    return pl.pallas_call(
        functools.partial(chunk_kernel, heads, mirrors, width),
        grid=(toks // block,),
        in_specs=[
            pl.BlockSpec((block, projected.shape[1]), lambda i: (i, 0)),
            pl.BlockSpec((block, gates), lambda i: (i, 0)),
            pl.BlockSpec((1, gates), lambda i: (0, 0)),
            pl.BlockSpec((1, gates), lambda i: (0, 0)),
        ],
        out_specs=[
            pl.BlockSpec((block, heads * width), lambda i: (i, 0)),
            pl.BlockSpec((block, heads * width), lambda i: (i, 0)),
            pl.BlockSpec((heads, 2 * width, width), lambda i: (0, 0, 0)),
        ],
        out_shape=[
            jax.ShapeDtypeStruct((toks, heads * width), F32),
            jax.ShapeDtypeStruct((toks, heads * width), F32),
            jax.ShapeDtypeStruct((heads, 2 * width, width), F32),
        ],
        compiler_params=pltpu.CompilerParams(vmem_limit_bytes=48 * 2**20),
        cost_estimate=pl.CostEstimate(
            flops=2 * units * 60 * span * span * width, bytes_accessed=4 * projected.size, transcendentals=0
        ),
        interpret=interpret,
    )(projected, gate_inputs, bias_row, rate_row)


def relay_kernel(heads, width, pre_ref, reach_ref, total_ref, out_ref, inbox, outbox, send_sem, recv_sem):
    me = lax.axis_index("ctx")
    group = lax.axis_index("head")
    count = lax.axis_size("ctx")
    first = me == 0
    final = me == count - 1
    barrier = pltpu.get_barrier_semaphore()

    def greet(other):
        pl.semaphore_signal(barrier, inc=1, device_id=(other, group), device_id_type=pl.DeviceIdType.MESH)

    @pl.when(jnp.logical_not(first))
    def _():
        greet(me - 1)

    @pl.when(jnp.logical_not(final))
    def _():
        greet(me + 1)

    edge = jnp.logical_or(first, final)

    @pl.when(edge)
    def _():
        pl.semaphore_wait(barrier, 1)

    @pl.when(jnp.logical_not(edge))
    def _():
        pl.semaphore_wait(barrier, 2)

    def copy(head):
        return pltpu.make_async_remote_copy(
            src_ref=outbox.at[head],
            dst_ref=inbox.at[head],
            send_sem=send_sem.at[head],
            recv_sem=recv_sem.at[head],
            device_id=(lax.rem(me + 1, count), group),
            device_id_type=pl.DeviceIdType.MESH,
        )

    @pl.when(first)
    def _():
        for head in range(heads):
            inbox[head] = jnp.zeros((width, width), F32)
            outbox[head] = total_ref[head, width:]
            copy(head).start()

    @pl.when(jnp.logical_not(first))
    def _():
        for head in range(heads):
            copy(head).wait_recv()

            @pl.when(jnp.logical_not(final))
            def _():
                outbox[head] = dot3(inbox[head], total_ref[head, :width]) + total_ref[head, width:]
                copy(head).start()

    for head in range(heads):
        cols = slice(head * width, (head + 1) * width)
        out = pre_ref[:, cols] + dot3(reach_ref[:, cols], inbox[head], NT)
        scale = lax.rsqrt(jnp.mean(out * out, axis=-1, keepdims=True) + 1e-06)
        out_ref[:, cols] = (out * scale).astype(BF16)

    @pl.when(jnp.logical_not(final))
    def _():
        for head in range(heads):
            copy(head).wait_send()


def relay_call(pre, reach, total, heads, width):
    return pl.pallas_call(
        functools.partial(relay_kernel, heads, width),
        out_shape=jax.ShapeDtypeStruct(pre.shape, BF16),
        in_specs=[pl.BlockSpec(memory_space=pltpu.VMEM)] * 3,
        out_specs=pl.BlockSpec(memory_space=pltpu.VMEM),
        scratch_shapes=[
            pltpu.VMEM((heads, width, width), F32),
            pltpu.VMEM((heads, width, width), F32),
            pltpu.SemaphoreType.DMA((heads,)),
            pltpu.SemaphoreType.DMA((heads,)),
        ],
        compiler_params=pltpu.CompilerParams(
            collective_id=0, has_side_effects=True, vmem_limit_bytes=32 * 2**20
        ),
        cost_estimate=pl.CostEstimate(
            flops=6 * pre.size * width, bytes_accessed=10 * pre.size, transcendentals=0
        ),
    )(pre, reach, total)


def gate_rows(beta_bias, decay_rate):
    heads, mirrors = beta_bias.shape
    bias = jnp.concatenate([beta_bias, jnp.zeros((heads, 1), F32)], axis=1).reshape(1, -1)
    rate = jnp.concatenate([jnp.zeros((heads, mirrors), F32), decay_rate[:, None]], axis=1).reshape(1, -1)
    return bias, rate


def shards(tokens, w_proj, w_small, beta_bias, decay_rate, w_out):
    tok_rows = tokens.shape[0]
    heads_here, mirrors = beta_bias.shape
    head_width = w_proj.shape[1] // (heads_here * (1 + 2 * mirrors))
    wide = w_proj.shape[1]
    fill = -w_small.shape[1] % 128
    both = jnp.concatenate([w_proj, jnp.pad(w_small, ((0, 0), (0, fill)))], axis=1)
    both = lax.all_gather(both, "ctx", axis=0, tiled=True)
    projected = jnp.dot(tokens, both, preferred_element_type=F32)
    grouped = lax.all_gather(w_out, "head", axis=0, tiled=True)
    grouped, projected = lax.optimization_barrier((grouped, projected))
    gate_inputs = projected[:, wide : wide + w_small.shape[1]]
    projected = projected[:, :wide]
    bias_row, rate_row = gate_rows(beta_bias, decay_rate)
    pre, reach, total = chunk_call(
        projected, gate_inputs, bias_row, rate_row, heads_here, mirrors, head_width
    )
    mixed_heads = relay_call(pre, reach, total, heads_here, head_width)
    full_out = lax.all_gather(grouped, "ctx", axis=1, tiled=True)
    group_count = lax.axis_size("head")
    rows_each = tok_rows // group_count
    stacked = mixed_heads.reshape(group_count, rows_each, heads_here * head_width)
    mixed = jnp.einsum(
        "irk,kd->ird",
        lax.all_to_all(stacked, "head", split_axis=0, concat_axis=2, tiled=True),
        full_out,
        preferred_element_type=F32,
    ).astype(BF16)
    return mixed.reshape(rows_each, full_out.shape[1])


def solution(mesh):
    placed = (
        P("ctx", None),
        P("ctx", "head"),
        P("ctx", "head"),
        P("head", None),
        P("head"),
        P("head", "ctx"),
    )
    return jax.shard_map(
        shards, mesh=mesh, in_specs=placed, out_specs=P(("ctx", "head"), None), check_vma=False
    )
```

```python
import functools
import math

import jax
import jax.numpy as jnp
from jax import lax
from jax.experimental import pallas as pl
from jax.experimental.pallas import tpu as pltpu
from jax.sharding import PartitionSpec as P

F32 = jnp.float32
BF16 = jnp.bfloat16
NN = (((1,), (0,)), ((), ()))
NT = (((1,), (1,)), ((), ()))
TN = (((0,), (0,)), ((), ()))
BLOCK = 64
BASE = 8


def dot1(left, right, dims=NN):
    return lax.dot_general(left, right, dims, preferred_element_type=F32)


def halves(array):
    high = array.astype(BF16)
    return high, (array - high.astype(F32)).astype(BF16)


def dot3(left, right, dims=NN):
    left_high, left_low = halves(left)
    right_high, right_low = halves(right)
    return (
        dot1(left_high, right_high, dims)
        + dot1(left_high, right_low, dims)
        + dot1(left_low, right_high, dims)
    )


def unit(vectors):
    return vectors * lax.rsqrt(jnp.sum(vectors * vectors, axis=-1, keepdims=True) + 1e-06)


def chunk_kernel(heads, mirrors, width, gate_at, proj_ref, gate_ref, bias_ref, rate_ref, pre_ref, reach_ref, total_ref):
    toks = proj_ref.shape[0]
    span = toks * mirrors
    parts = 1 + 2 * mirrors
    gates = mirrors + 1

    @pl.when(pl.program_id(0) == 0)
    def _():
        rows = lax.broadcasted_iota(jnp.int32, (2 * width, width), 0)
        cols = lax.broadcasted_iota(jnp.int32, (2 * width, width), 1)
        start = jnp.where(rows == cols, 1.0, 0.0).astype(F32)
        for head in range(heads):
            total_ref[head] = start

    gate = gate_ref[...]
    strength = 2.0 / (1.0 + jnp.exp(-(gate + bias_ref[...])))
    log_decay = -rate_ref[...] * (jnp.maximum(gate, 0.0) + jnp.log(1.0 + jnp.exp(-jnp.abs(gate))))
    tok_r = lax.broadcasted_iota(jnp.int32, (toks, toks), 0)
    tok_c = lax.broadcasted_iota(jnp.int32, (toks, toks), 1)
    upto = jnp.where(tok_r >= tok_c, 1.0, 0.0).astype(F32)
    summed = lax.dot_general(
        upto, log_decay, NN, precision=lax.Precision.HIGHEST, preferred_element_type=F32
    )
    step_r = lax.broadcasted_iota(jnp.int32, (span, span), 0)
    step_c = lax.broadcasted_iota(jnp.int32, (span, span), 1)
    place_r = (step_r % toks) * mirrors + step_r // toks
    place_c = (step_c % toks) * mirrors + step_c // toks
    strict = place_r > place_c
    diagonal = step_r == step_c
    eye = jnp.where(diagonal, 1.0, 0.0).astype(F32)
    see_r = lax.broadcasted_iota(jnp.int32, (toks, span), 0)
    see_c = lax.broadcasted_iota(jnp.int32, (toks, span), 1)
    visible = see_c % toks <= see_r

    each = range(heads)

    def part(head, index):
        at = (head * parts + index) * width
        return proj_ref[:, at : at + width]

    query = [unit(part(h, 0)) for h in each]
    keys = [jnp.concatenate([unit(part(h, 1 + r)) for r in range(mirrors)], axis=0) for h in each]
    values = [jnp.concatenate([part(h, 1 + mirrors + r) for r in range(mirrors)], axis=0) for h in each]
    beta = [
        jnp.concatenate([strength[:, gate_at + h * gates + r : gate_at + h * gates + r + 1] for r in range(mirrors)], axis=0)
        for h in each
    ]
    decay_at = [gate_at + h * gates + mirrors for h in each]
    run_q = [summed[:, decay_at[h] : decay_at[h] + 1] for h in each]
    run = [jnp.concatenate([run_q[h]] * mirrors, axis=0) for h in each]
    run_row = [jnp.sum(jnp.where(diagonal, run[h], 0.0), axis=0, keepdims=True) for h in each]
    last = [run_q[h][toks - 1 :, :] for h in each]
    inner = [dot3(jnp.concatenate([keys[h], query[h]], axis=0), keys[h], NT) for h in each]
    lower = [
        jnp.where(strict, beta[h] * jnp.exp(jnp.where(strict, run[h] - run_row[h], 0.0)) * inner[h][:span], 0.0)
        for h in each
    ]
    attend = [
        jnp.where(visible, jnp.exp(jnp.where(visible, run_q[h] - run_row[h], 0.0)) * inner[h][span:], 0.0)
        for h in each
    ]
    low_high = [halves(lower[h]) for h in each]
    near = place_r // BASE == place_c // BASE
    zero = jnp.zeros((), BF16)
    power = [jnp.where(near, low_high[h][0], zero) for h in each]
    inv = [eye - jnp.where(near, lower[h], 0.0) for h in each]
    reached = 2
    while reached < BASE:
        power = [dot1(power[h], power[h]).astype(BF16) for h in each]
        inv = [inv[h] + dot1(inv[h].astype(BF16), power[h]) for h in each]
        reached *= 2
    size = BASE
    while size < span:
        joined = (place_r // (2 * size) == place_c // (2 * size)) & (place_r // size != place_c // size)
        inv_now = [inv[h].astype(BF16) for h in each]
        cross = [dot1(jnp.where(joined, low_high[h][0], zero), inv_now[h]).astype(BF16) for h in each]
        inv = [inv[h] - dot1(inv_now[h], cross[h]) for h in each]
        size *= 2
    rough = [inv[h].astype(BF16) for h in each]
    left = [
        (eye - rough[h].astype(F32)) - dot1(low_high[h][0], rough[h]) - dot1(low_high[h][1], rough[h])
        for h in each
    ]
    inv = [rough[h].astype(F32) + dot1(rough[h], left[h].astype(BF16)) for h in each]
    left = [(eye - inv[h]) - dot3(lower[h], inv[h]) for h in each]
    inv = [inv[h] + dot1(rough[h], left[h].astype(BF16)) for h in each]

    given = [
        jnp.concatenate([beta[h] * values[h], (beta[h] * jnp.exp(run[h])) * keys[h]], axis=1) for h in each
    ]
    weighted = [dot3(inv[h], given[h]) for h in each]
    tails = [jnp.exp(last[h] - run[h]) * keys[h] for h in each]
    moved = [dot3(weighted[h], tails[h], TN) for h in each]
    seen = [dot3(attend[h], weighted[h]) for h in each]
    asked = [jnp.exp(run_q[h]) * query[h] - seen[h][:, width:] for h in each]
    before = [total_ref[h] for h in each]
    answers = [dot3(asked[h], before[h], NT) for h in each]
    after = [dot3(before[h], moved[h][width:]) for h in each]
    for h in each:
        reach_ref[:, h * width : (h + 1) * width] = answers[h][:, :width]
        pre_ref[:, h * width : (h + 1) * width] = answers[h][:, width:] + seen[h][:, :width]
        carried = jnp.exp(last[h]) * before[h] - after[h]
        total_ref[h, :width] = carried[:width]
        total_ref[h, width:] = carried[width:] + moved[h][:width]


def chunk_call(projected, gated, bias_row, rate_row, heads, mirrors, width, first_head, interpret=False):
    toks = projected.shape[0]
    block = math.gcd(toks, BLOCK)
    lanes = bias_row.shape[1]
    gate_block = gated.shape[1] // lanes - 1
    span = block * mirrors
    units = toks // block * heads
    return pl.pallas_call(
        functools.partial(chunk_kernel, heads, mirrors, width, first_head * (mirrors + 1)),
        grid=(toks // block,),
        in_specs=[
            pl.BlockSpec((block, heads * (1 + 2 * mirrors) * width), lambda i: (i, 0)),
            pl.BlockSpec((block, lanes), lambda i: (i, gate_block)),
            pl.BlockSpec((1, lanes), lambda i: (0, 0)),
            pl.BlockSpec((1, lanes), lambda i: (0, 0)),
        ],
        out_specs=[
            pl.BlockSpec((block, heads * width), lambda i: (i, 0)),
            pl.BlockSpec((block, heads * width), lambda i: (i, 0)),
            pl.BlockSpec((heads, 2 * width, width), lambda i: (0, 0, 0)),
        ],
        out_shape=[
            jax.ShapeDtypeStruct((toks, heads * width), F32),
            jax.ShapeDtypeStruct((toks, heads * width), F32),
            jax.ShapeDtypeStruct((heads, 2 * width, width), F32),
        ],
        compiler_params=pltpu.CompilerParams(vmem_limit_bytes=48 * 2**20),
        cost_estimate=pl.CostEstimate(
            flops=2 * units * 60 * span * span * width, bytes_accessed=4 * projected.size, transcendentals=0
        ),
        interpret=interpret,
    )(projected, gated, bias_row, rate_row)


def relay_kernel(heads, width, groups, *refs):
    out_ref, inbox, outbox, send_sem, recv_sem = refs[3 * groups :]
    each = heads // groups

    def total_of(head, rows):
        return refs[3 * (head // each) + 2][head % each, rows]

    me = lax.axis_index("ctx")
    group = lax.axis_index("head")
    count = lax.axis_size("ctx")
    first = me == 0
    final = me == count - 1
    barrier = pltpu.get_barrier_semaphore()

    def greet(other):
        pl.semaphore_signal(barrier, inc=1, device_id=(other, group), device_id_type=pl.DeviceIdType.MESH)

    @pl.when(jnp.logical_not(first))
    def _():
        greet(me - 1)

    @pl.when(jnp.logical_not(final))
    def _():
        greet(me + 1)

    edge = jnp.logical_or(first, final)

    @pl.when(edge)
    def _():
        pl.semaphore_wait(barrier, 1)

    @pl.when(jnp.logical_not(edge))
    def _():
        pl.semaphore_wait(barrier, 2)

    def copy(head):
        return pltpu.make_async_remote_copy(
            src_ref=outbox.at[head],
            dst_ref=inbox.at[head],
            send_sem=send_sem.at[head],
            recv_sem=recv_sem.at[head],
            device_id=(lax.rem(me + 1, count), group),
            device_id_type=pl.DeviceIdType.MESH,
        )

    @pl.when(first)
    def _():
        for head in range(heads):
            inbox[head] = jnp.zeros((width, width), F32)
            outbox[head] = total_of(head, slice(width, None))
            copy(head).start()

    @pl.when(jnp.logical_not(first))
    def _():
        for head in range(heads):
            copy(head).wait_recv()

            @pl.when(jnp.logical_not(final))
            def _():
                outbox[head] = dot3(inbox[head], total_of(head, slice(0, width))) + total_of(
                    head, slice(width, None)
                )
                copy(head).start()

    for head in range(heads):
        cols = slice(head * width, (head + 1) * width)
        pre_ref, reach_ref = refs[3 * (head // each) : 3 * (head // each) + 2]
        own = slice(head % each * width, (head % each + 1) * width)
        out = pre_ref[:, own] + dot3(reach_ref[:, own], inbox[head], NT)
        scale = lax.rsqrt(jnp.mean(out * out, axis=-1, keepdims=True) + 1e-06)
        out_ref[:, cols] = (out * scale).astype(BF16)

    @pl.when(jnp.logical_not(final))
    def _():
        for head in range(heads):
            copy(head).wait_send()


def relay_call(worked, heads, width):
    flat = [array for group in worked for array in group]
    toks = worked[0][0].shape[0]
    size = toks * heads * width
    return pl.pallas_call(
        functools.partial(relay_kernel, heads, width, len(worked)),
        out_shape=jax.ShapeDtypeStruct((toks, heads * width), BF16),
        in_specs=[pl.BlockSpec(memory_space=pltpu.VMEM)] * len(flat),
        out_specs=pl.BlockSpec(memory_space=pltpu.VMEM),
        scratch_shapes=[
            pltpu.VMEM((heads, width, width), F32),
            pltpu.VMEM((heads, width, width), F32),
            pltpu.SemaphoreType.DMA((heads,)),
            pltpu.SemaphoreType.DMA((heads,)),
        ],
        compiler_params=pltpu.CompilerParams(
            collective_id=0, has_side_effects=True, vmem_limit_bytes=32 * 2**20
        ),
        cost_estimate=pl.CostEstimate(
            flops=6 * size * width, bytes_accessed=10 * size, transcendentals=0
        ),
    )(*flat)


def gate_rows(beta_bias, decay_rate):
    heads, mirrors = beta_bias.shape
    fill = ((0, 0), (0, -heads * (mirrors + 1) % 128))
    bias = jnp.concatenate([beta_bias, jnp.zeros((heads, 1), F32)], axis=1).reshape(1, -1)
    rate = jnp.concatenate([jnp.zeros((heads, mirrors), F32), decay_rate[:, None]], axis=1).reshape(1, -1)
    return jnp.pad(bias, fill), jnp.pad(rate, fill)


def shards(tokens, w_proj, w_small, beta_bias, decay_rate, w_out):
    tok_rows = tokens.shape[0]
    heads_here, mirrors = beta_bias.shape
    head_width = w_proj.shape[1] // (heads_here * (1 + 2 * mirrors))
    groups = math.gcd(heads_here, 2)
    each = heads_here // groups
    wide = w_proj.shape[1] // groups
    small = jnp.pad(w_small, ((0, 0), (0, -w_small.shape[1] % 128)))
    bias_row, rate_row = gate_rows(beta_bias, decay_rate)
    held = jnp.concatenate([w_proj[:, :wide], small], axis=1)
    first_projected = None
    worked = []
    for group in range(groups):
        full = lax.all_gather(held, "ctx", axis=0, tiled=True)
        if group + 1 < groups:
            held = w_proj[:, (group + 1) * wide : (group + 2) * wide]
            held, w_out, full = lax.optimization_barrier((held, w_out, full))
        if group == 0:
            grouped = lax.all_gather(w_out, "ctx", axis=1, tiled=True)
        else:
            tokens, _ = lax.optimization_barrier((tokens, worked[-1][2]))
        projected = jnp.dot(tokens, full, preferred_element_type=F32)
        if group == 0:
            first_projected = projected
        if group + 1 == groups:
            grouped, projected = lax.optimization_barrier((grouped, projected))
            if groups == 1:
                first_projected = projected
        worked.append(
            chunk_call(
                projected, first_projected, bias_row, rate_row, each, mirrors, head_width, group * each
            )
        )
    mixed_heads = relay_call(worked, heads_here, head_width)
    full_out = lax.all_gather(grouped, "head", axis=0, tiled=True)
    group_count = lax.axis_size("head")
    rows_each = tok_rows // group_count
    stacked = mixed_heads.reshape(group_count, rows_each, heads_here * head_width)
    mixed = jnp.einsum(
        "irk,kd->ird",
        lax.all_to_all(stacked, "head", split_axis=0, concat_axis=2, tiled=True),
        full_out,
        preferred_element_type=F32,
    ).astype(BF16)
    return mixed.reshape(rows_each, full_out.shape[1])


def solution(mesh):
    placed = (
        P("ctx", None),
        P("ctx", "head"),
        P("ctx", "head"),
        P("head", None),
        P("head"),
        P("head", "ctx"),
    )
    return jax.shard_map(
        shards, mesh=mesh, in_specs=placed, out_specs=P(("ctx", "head"), None), check_vma=False
    )
```

```python
import functools
import math

import jax
import jax.numpy as jnp
from jax import lax
from jax.experimental import pallas as pl
from jax.experimental.pallas import tpu as pltpu
from jax.sharding import PartitionSpec as P

F32 = jnp.float32
BF16 = jnp.bfloat16
NN = (((1,), (0,)), ((), ()))
NT = (((1,), (1,)), ((), ()))
TN = (((0,), (0,)), ((), ()))
BLOCK = 64
BASE = 8


def dot1(left, right, dims=NN):
    return lax.dot_general(left, right, dims, preferred_element_type=F32)


def halves(array):
    high = array.astype(BF16)
    return high, (array - high.astype(F32)).astype(BF16)


def dot3(left, right, dims=NN):
    left_high, left_low = halves(left)
    right_high, right_low = halves(right)
    return (
        dot1(left_high, right_high, dims)
        + dot1(left_high, right_low, dims)
        + dot1(left_low, right_high, dims)
    )


def unit(vectors):
    return vectors * lax.rsqrt(jnp.sum(vectors * vectors, axis=-1, keepdims=True) + 1e-06)


def chunk_kernel(heads, mirrors, width, gate_at, proj_ref, gate_ref, bias_ref, rate_ref, pre_ref, reach_ref, total_ref):
    toks = proj_ref.shape[0]
    span = toks * mirrors
    parts = 1 + 2 * mirrors
    gates = mirrors + 1

    @pl.when(pl.program_id(0) == 0)
    def _():
        rows = lax.broadcasted_iota(jnp.int32, (2 * width, width), 0)
        cols = lax.broadcasted_iota(jnp.int32, (2 * width, width), 1)
        start = jnp.where(rows == cols, 1.0, 0.0).astype(F32)
        for head in range(heads):
            total_ref[head] = start

    gate = gate_ref[...]
    strength = 2.0 / (1.0 + jnp.exp(-(gate + bias_ref[...])))
    log_decay = -rate_ref[...] * (jnp.maximum(gate, 0.0) + jnp.log(1.0 + jnp.exp(-jnp.abs(gate))))
    tok_r = lax.broadcasted_iota(jnp.int32, (toks, toks), 0)
    tok_c = lax.broadcasted_iota(jnp.int32, (toks, toks), 1)
    upto = jnp.where(tok_r >= tok_c, 1.0, 0.0).astype(F32)
    summed = lax.dot_general(
        upto, log_decay, NN, precision=lax.Precision.HIGHEST, preferred_element_type=F32
    )
    step_r = lax.broadcasted_iota(jnp.int32, (span, span), 0)
    step_c = lax.broadcasted_iota(jnp.int32, (span, span), 1)
    place_r = (step_r % toks) * mirrors + step_r // toks
    place_c = (step_c % toks) * mirrors + step_c // toks
    strict = place_r > place_c
    diagonal = step_r == step_c
    eye = jnp.where(diagonal, 1.0, 0.0).astype(F32)
    see_r = lax.broadcasted_iota(jnp.int32, (toks, span), 0)
    see_c = lax.broadcasted_iota(jnp.int32, (toks, span), 1)
    visible = see_c % toks <= see_r

    each = range(heads)

    def part(head, index):
        at = (head * parts + index) * width
        return proj_ref[:, at : at + width]

    query = [unit(part(h, 0)) for h in each]
    keys = [jnp.concatenate([unit(part(h, 1 + r)) for r in range(mirrors)], axis=0) for h in each]
    values = [jnp.concatenate([part(h, 1 + mirrors + r) for r in range(mirrors)], axis=0) for h in each]
    beta = [
        jnp.concatenate([strength[:, gate_at + h * gates + r : gate_at + h * gates + r + 1] for r in range(mirrors)], axis=0)
        for h in each
    ]
    decay_at = [gate_at + h * gates + mirrors for h in each]
    run_q = [summed[:, decay_at[h] : decay_at[h] + 1] for h in each]
    run = [jnp.concatenate([run_q[h]] * mirrors, axis=0) for h in each]
    run_row = [jnp.sum(jnp.where(diagonal, run[h], 0.0), axis=0, keepdims=True) for h in each]
    last = [run_q[h][toks - 1 :, :] for h in each]
    inner = [dot3(jnp.concatenate([keys[h], query[h]], axis=0), keys[h], NT) for h in each]
    lower = [
        jnp.where(strict, beta[h] * jnp.exp(jnp.where(strict, run[h] - run_row[h], 0.0)) * inner[h][:span], 0.0)
        for h in each
    ]
    attend = [
        jnp.where(visible, jnp.exp(jnp.where(visible, run_q[h] - run_row[h], 0.0)) * inner[h][span:], 0.0)
        for h in each
    ]
    low_high = [halves(lower[h]) for h in each]
    near = place_r // BASE == place_c // BASE
    zero = jnp.zeros((), BF16)
    power = [jnp.where(near, low_high[h][0], zero) for h in each]
    inv = [eye - jnp.where(near, lower[h], 0.0) for h in each]
    reached = 2
    while reached < BASE:
        power = [dot1(power[h], power[h]).astype(BF16) for h in each]
        inv = [inv[h] + dot1(inv[h].astype(BF16), power[h]) for h in each]
        reached *= 2
    size = BASE
    while size < span:
        joined = (place_r // (2 * size) == place_c // (2 * size)) & (place_r // size != place_c // size)
        inv_now = [inv[h].astype(BF16) for h in each]
        cross = [dot1(jnp.where(joined, low_high[h][0], zero), inv_now[h]).astype(BF16) for h in each]
        inv = [inv[h] - dot1(inv_now[h], cross[h]) for h in each]
        size *= 2
    rough = [inv[h].astype(BF16) for h in each]
    left = [
        (eye - rough[h].astype(F32)) - dot1(low_high[h][0], rough[h]) - dot1(low_high[h][1], rough[h])
        for h in each
    ]
    inv = [rough[h].astype(F32) + dot1(rough[h], left[h].astype(BF16)) for h in each]
    left = [(eye - inv[h]) - dot3(lower[h], inv[h]) for h in each]
    inv = [inv[h] + dot1(rough[h], left[h].astype(BF16)) for h in each]

    given = [
        jnp.concatenate([beta[h] * values[h], (beta[h] * jnp.exp(run[h])) * keys[h]], axis=1) for h in each
    ]
    weighted = [dot3(inv[h], given[h]) for h in each]
    tails = [jnp.exp(last[h] - run[h]) * keys[h] for h in each]
    moved = [dot3(weighted[h], tails[h], TN) for h in each]
    seen = [dot3(attend[h], weighted[h]) for h in each]
    asked = [jnp.exp(run_q[h]) * query[h] - seen[h][:, width:] for h in each]
    before = [total_ref[h] for h in each]
    answers = [dot3(asked[h], before[h], NT) for h in each]
    after = [dot3(before[h], moved[h][width:]) for h in each]
    for h in each:
        reach_ref[:, h * width : (h + 1) * width] = answers[h][:, :width]
        pre_ref[:, h * width : (h + 1) * width] = answers[h][:, width:] + seen[h][:, :width]
        carried = jnp.exp(last[h]) * before[h] - after[h]
        total_ref[h, :width] = carried[:width]
        total_ref[h, width:] = carried[width:] + moved[h][:width]


def chunk_call(projected, gated, bias_row, rate_row, heads, mirrors, width, first_head, interpret=False):
    toks = projected.shape[0]
    block = math.gcd(toks, BLOCK)
    lanes = bias_row.shape[1]
    gate_block = gated.shape[1] // lanes - 1
    span = block * mirrors
    units = toks // block * heads
    return pl.pallas_call(
        functools.partial(chunk_kernel, heads, mirrors, width, first_head * (mirrors + 1)),
        grid=(toks // block,),
        in_specs=[
            pl.BlockSpec((block, heads * (1 + 2 * mirrors) * width), lambda i: (i, 0)),
            pl.BlockSpec((block, lanes), lambda i: (i, gate_block)),
            pl.BlockSpec((1, lanes), lambda i: (0, 0)),
            pl.BlockSpec((1, lanes), lambda i: (0, 0)),
        ],
        out_specs=[
            pl.BlockSpec((block, heads * width), lambda i: (i, 0)),
            pl.BlockSpec((block, heads * width), lambda i: (i, 0)),
            pl.BlockSpec((heads, 2 * width, width), lambda i: (0, 0, 0)),
        ],
        out_shape=[
            jax.ShapeDtypeStruct((toks, heads * width), F32),
            jax.ShapeDtypeStruct((toks, heads * width), F32),
            jax.ShapeDtypeStruct((heads, 2 * width, width), F32),
        ],
        compiler_params=pltpu.CompilerParams(vmem_limit_bytes=48 * 2**20),
        cost_estimate=pl.CostEstimate(
            flops=2 * units * 60 * span * span * width, bytes_accessed=4 * projected.size, transcendentals=0
        ),
        interpret=interpret,
    )(projected, gated, bias_row, rate_row)


def relay_kernel(heads, width, groups, *refs):
    out_ref, inbox, outbox, send_sem, recv_sem = refs[3 * groups :]
    each = heads // groups

    def total_of(head, rows):
        return refs[3 * (head // each) + 2][head % each, rows]

    me = lax.axis_index("ctx")
    group = lax.axis_index("head")
    count = lax.axis_size("ctx")
    first = me == 0
    final = me == count - 1
    barrier = pltpu.get_barrier_semaphore()

    def greet(other):
        pl.semaphore_signal(barrier, inc=1, device_id=(other, group), device_id_type=pl.DeviceIdType.MESH)

    @pl.when(jnp.logical_not(first))
    def _():
        greet(me - 1)

    @pl.when(jnp.logical_not(final))
    def _():
        greet(me + 1)

    edge = jnp.logical_or(first, final)

    @pl.when(edge)
    def _():
        pl.semaphore_wait(barrier, 1)

    @pl.when(jnp.logical_not(edge))
    def _():
        pl.semaphore_wait(barrier, 2)

    def copy(head):
        return pltpu.make_async_remote_copy(
            src_ref=outbox.at[head],
            dst_ref=inbox.at[head],
            send_sem=send_sem.at[head],
            recv_sem=recv_sem.at[head],
            device_id=(lax.rem(me + 1, count), group),
            device_id_type=pl.DeviceIdType.MESH,
        )

    @pl.when(first)
    def _():
        for head in range(heads):
            inbox[head] = jnp.zeros((width, width), F32)
            outbox[head] = total_of(head, slice(width, None))
            copy(head).start()

    @pl.when(jnp.logical_not(first))
    def _():
        for head in range(heads):
            copy(head).wait_recv()

            @pl.when(jnp.logical_not(final))
            def _():
                outbox[head] = dot3(inbox[head], total_of(head, slice(0, width))) + total_of(
                    head, slice(width, None)
                )
                copy(head).start()

    for head in range(heads):
        cols = slice(head * width, (head + 1) * width)
        pre_ref, reach_ref = refs[3 * (head // each) : 3 * (head // each) + 2]
        own = slice(head % each * width, (head % each + 1) * width)
        out = pre_ref[:, own] + dot3(reach_ref[:, own], inbox[head], NT)
        scale = lax.rsqrt(jnp.mean(out * out, axis=-1, keepdims=True) + 1e-06)
        out_ref[:, cols] = (out * scale).astype(BF16)

    @pl.when(jnp.logical_not(final))
    def _():
        for head in range(heads):
            copy(head).wait_send()


def relay_call(worked, heads, width):
    flat = [array for group in worked for array in group]
    toks = worked[0][0].shape[0]
    size = toks * heads * width
    return pl.pallas_call(
        functools.partial(relay_kernel, heads, width, len(worked)),
        out_shape=jax.ShapeDtypeStruct((toks, heads * width), BF16),
        in_specs=[pl.BlockSpec(memory_space=pltpu.VMEM)] * len(flat),
        out_specs=pl.BlockSpec(memory_space=pltpu.VMEM),
        scratch_shapes=[
            pltpu.VMEM((heads, width, width), F32),
            pltpu.VMEM((heads, width, width), F32),
            pltpu.SemaphoreType.DMA((heads,)),
            pltpu.SemaphoreType.DMA((heads,)),
        ],
        compiler_params=pltpu.CompilerParams(
            collective_id=0, has_side_effects=True, vmem_limit_bytes=32 * 2**20
        ),
        cost_estimate=pl.CostEstimate(
            flops=6 * size * width, bytes_accessed=10 * size, transcendentals=0
        ),
    )(*flat)


def gate_rows(beta_bias, decay_rate):
    heads, mirrors = beta_bias.shape
    fill = ((0, 0), (0, -heads * (mirrors + 1) % 128))
    bias = jnp.concatenate([beta_bias, jnp.zeros((heads, 1), F32)], axis=1).reshape(1, -1)
    rate = jnp.concatenate([jnp.zeros((heads, mirrors), F32), decay_rate[:, None]], axis=1).reshape(1, -1)
    return jnp.pad(bias, fill), jnp.pad(rate, fill)


def permuted_columns(block, axis):
    count = lax.axis_size(axis)
    me = lax.axis_index(axis)
    rows, cols = block.shape
    placed = lax.dynamic_update_slice(jnp.zeros((count, rows, cols), block.dtype), block[None], (me, 0, 0))
    for by in range(1, count):
        piece = lax.ppermute(block, axis, [(i, (i + by) % count) for i in range(count)])
        placed = lax.dynamic_update_slice(placed, piece[None], (lax.rem(me + count - by, count), 0, 0))
    return jnp.moveaxis(placed, 0, 1).reshape(rows, count * cols)


def shards(tokens, w_proj, w_small, beta_bias, decay_rate, w_out):
    tok_rows = tokens.shape[0]
    heads_here, mirrors = beta_bias.shape
    head_width = w_proj.shape[1] // (heads_here * (1 + 2 * mirrors))
    groups = 1
    each = heads_here // groups
    wide = w_proj.shape[1] // groups
    small = jnp.pad(w_small, ((0, 0), (0, -w_small.shape[1] % 128)))
    bias_row, rate_row = gate_rows(beta_bias, decay_rate)
    held = jnp.concatenate([w_proj[:, :wide], small], axis=1)
    first_projected = None
    worked = []
    for group in range(groups):
        full = lax.all_gather(held, "ctx", axis=0, tiled=True)
        if group + 1 < groups:
            held = w_proj[:, (group + 1) * wide : (group + 2) * wide]
            held, w_out, full = lax.optimization_barrier((held, w_out, full))
        if group == 0:
            grouped = permuted_columns(w_out, "ctx")
        else:
            tokens, _ = lax.optimization_barrier((tokens, worked[-1][2]))
        projected = jnp.dot(tokens, full, preferred_element_type=F32)
        if group == 0:
            first_projected = projected
        if group + 1 == groups:
            grouped, projected = lax.optimization_barrier((grouped, projected))
            if groups == 1:
                first_projected = projected
        worked.append(
            chunk_call(
                projected, first_projected, bias_row, rate_row, each, mirrors, head_width, group * each
            )
        )
    mixed_heads = relay_call(worked, heads_here, head_width)
    full_out = lax.all_gather(grouped, "head", axis=0, tiled=True)
    group_count = lax.axis_size("head")
    rows_each = tok_rows // group_count
    stacked = mixed_heads.reshape(group_count, rows_each, heads_here * head_width)
    mixed = jnp.einsum(
        "irk,kd->ird",
        lax.all_to_all(stacked, "head", split_axis=0, concat_axis=2, tiled=True),
        full_out,
        preferred_element_type=F32,
    ).astype(BF16)
    return mixed.reshape(rows_each, full_out.shape[1])


def solution(mesh):
    placed = (
        P("ctx", None),
        P("ctx", "head"),
        P("ctx", "head"),
        P("head", None),
        P("head"),
        P("head", "ctx"),
    )
    return jax.shard_map(
        shards, mesh=mesh, in_specs=placed, out_specs=P(("ctx", "head"), None), check_vma=False
    )
```
